32 devices in a mesh: seq: 16 (over z, y, core), head: 2 (over x).
Axes of the slice: x: 2, y: 2, z: 4, core: 2. Of those that a mesh axis runs over, the one named last changes fastest.
Arguments:
- queries: bfloat16 [2, 4096, 2048], P(None, 'seq', 'head'), may hold values from -8 to 8
- key_states: bfloat16 [2, 4096, 2048], P(None, 'seq', 'head'), may hold values from -8 to 8
- value_states: bfloat16 [2, 4096, 2048], P(None, 'seq', 'head'), may hold values from -6 to 6
- output_grad: bfloat16 [2, 4096, 2048], P(None, 'seq', 'head'), may hold values from -6 to 6
- out_proj: bfloat16 [2048, 2048], P('head'), may hold values from -0.125 to 0.125
Outputs:
- layer_out: bfloat16 [2, 4096, 2048], P(None, 'seq', 'head')
- query_grad: bfloat16 [2, 4096, 2048], P(None, 'seq', 'head')
- key_grad: bfloat16 [2, 4096, 2048], P(None, 'seq', 'head')
- value_grad: bfloat16 [2, 4096, 2048], P(None, 'seq', 'head')
The draws below stay inside these ranges and needn't reach their ends.
All inputs are finite; a program needn't handle non-finite values.
Results may differ from the reference program's by a relative error of at most 0.012.
The reference program's roundings to bfloat16 on the way count: a program that leaves them out, or rounds other values in their place, can miss the bound.
Values may be sent and summed in bfloat16 or wider, within the bound.
No kernel may reach another device: no remote copies, remote signals or barrier semaphores. Data moves between devices by JAX's collectives and lax.ppermute only.
A program may use at most 192 MiB of HBM per device.

```python
import jax
import jax.numpy as jnp
from jax import lax

HEADS = 16
HEAD_DIM = 128
BLOCK = 256
BATCH = 2
SEQ = 4096
N_SEQ = 16


def base_draw(key, salt):
    full_shape = (BATCH, SEQ, HEADS * HEAD_DIM)
    return jnp.clip(jax.random.normal(jax.random.fold_in(key, salt), full_shape, jnp.float32), -4.0, 4.0)


def draw_queries(key, part):
    drawn = base_draw(key, 1)
    return drawn.astype(jnp.bfloat16)


def draw_key_states(key, part):
    drawn = base_draw(key, 2)
    return drawn.astype(jnp.bfloat16)


def steps_of(stream_key, dims, pieces, smallest, high):
    loudness, own = 1.0, jax.random.fold_in(stream_key, 6)
    for axis_at, shards_of in pieces:
        draws = jnp.exp(jax.random.uniform(jax.random.fold_in(own, axis_at), (shards_of,), jnp.float32, smallest / len(pieces), high / len(pieces)))
        loudness = loudness * jnp.repeat(draws, dims[axis_at] // shards_of).reshape([-1 if axis == axis_at else 1 for axis in range(len(dims))])
    return loudness


def scatter_about(own_key, shape, deviation, reach, shards=(), kind=jnp.bfloat16):
    gain = steps_of(own_key, shape, shards, -0.22, 0.18) if shards else 1.0
    drawn = jax.random.normal(own_key, shape, jnp.float32) * deviation * gain
    return jnp.minimum(jnp.maximum(drawn, -reach), reach).astype(kind)


def setup_inputs(seed: int = 0) -> dict:
    key_list = jax.random.split(jax.random.key(seed), 6)
    return {
        "queries": draw_queries(jax.random.fold_in(key_list[5], 71), 0),
        "key_states": draw_key_states(jax.random.fold_in(key_list[5], 71), 0),
        "value_states": scatter_about(key_list[2], (BATCH, SEQ, HEADS * HEAD_DIM), 1.0, 6.0, ((1, 16), (2, 2))),
        "output_grad": scatter_about(key_list[3], (BATCH, SEQ, HEADS * HEAD_DIM), 1.0, 6.0, ((1, 16), (2, 2))),
        "out_proj": scatter_about(key_list[4], (HEADS * HEAD_DIM, HEADS * HEAD_DIM), (HEADS * HEAD_DIM) ** -0.5, 0.125, ((0, 2),)),
    }


def rounded(value):
    return lax.optimization_barrier(value.astype(jnp.bfloat16)).astype(jnp.float32)


def reference(queries, key_states, value_states, output_grad, out_proj):
    score_scale = HEAD_DIM ** -0.5
    levels = N_SEQ.bit_length() - 1
    width = HEADS * HEAD_DIM
    batch = queries.shape[0]
    num_blocks = SEQ // BLOCK
    attn_flat = jnp.dot(output_grad.reshape(-1, width), out_proj.T, preferred_element_type=jnp.float32)
    attn_grad = attn_flat.astype(jnp.bfloat16).reshape(batch, SEQ, width)
    causal = jnp.arange(BLOCK)[:, None] >= jnp.arange(BLOCK)[None, :]

    def rows_of(source, block_index):
        start = (block_index * BLOCK).astype(jnp.int32)
        piece = lax.dynamic_slice_in_dim(source, start, BLOCK, 1)
        return piece.reshape(batch, BLOCK, HEADS, HEAD_DIM).astype(jnp.float32)

    def add_rows(total, block_index, term):
        start = (block_index * BLOCK).astype(jnp.int32)
        current = lax.dynamic_slice_in_dim(total, start, BLOCK, 1)
        return lax.dynamic_update_slice_in_dim(total, current + term, start, 1)

    def one_block(block_index, state_tuple):
        attention, query_grad, key_total, value_total = state_tuple
        block_index = jnp.asarray(block_index).astype(jnp.int32)
        partners = [jnp.bitwise_xor(block_index, 1 << depth_index).astype(jnp.int32) for depth_index in range(levels)]
        seen = [block_index] + partners
        key_row_block = jnp.concatenate([rows_of(key_states, item) for item in seen], axis=1)
        value_row_block = jnp.concatenate([rows_of(value_states, item) for item in seen], axis=1)
        query_row_block = rows_of(queries, block_index)
        gradient_row_block = rows_of(attn_grad, block_index)
        key_mask = jnp.concatenate([causal] + [jnp.broadcast_to(item < block_index, (BLOCK, BLOCK)) for item in partners], axis=1)
        scores = jnp.einsum('bqhd,bkhd->bhqk', query_row_block, key_row_block) * score_scale
        scores = jnp.where(key_mask, scores, -jnp.inf)
        maxima = jnp.max(scores, axis=3, keepdims=True)
        log_norm = maxima + jnp.log(jnp.sum(jnp.exp(scores - maxima), axis=3, keepdims=True))
        weights = jnp.exp(scores - log_norm)
        lower_weight_block = rounded(weights)
        attn_block = jnp.einsum('bhqk,bkhd->bqhd', lower_weight_block, value_row_block).astype(jnp.bfloat16)
        row_dsum = jnp.sum(gradient_row_block * attn_block.astype(jnp.float32), axis=3)
        grad_weights = jnp.einsum('bqhd,bkhd->bhqk', gradient_row_block, value_row_block)
        score_gradients = rounded(weights * (grad_weights - jnp.transpose(row_dsum, (0, 2, 1))[..., None]))
        dquery = (jnp.einsum('bhqk,bkhd->bqhd', score_gradients, key_row_block) * score_scale).astype(jnp.bfloat16)
        key_term = jnp.einsum('bhqk,bqhd->bkhd', score_gradients, query_row_block) * score_scale
        value_term = jnp.einsum('bhqk,bqhd->bkhd', lower_weight_block, gradient_row_block)
        start = (block_index * BLOCK).astype(jnp.int32)
        attention = lax.dynamic_update_slice_in_dim(attention, attn_block, start, 1)
        query_grad = lax.dynamic_update_slice_in_dim(query_grad, dquery, start, 1)
        key_total = add_rows(key_total, block_index, key_term[:, :BLOCK])
        value_total = add_rows(value_total, block_index, value_term[:, :BLOCK])
        for depth_index in range(levels):
            low = (depth_index + 1) * BLOCK
            key_total = add_rows(key_total, partners[depth_index], rounded(key_term[:, low:low + BLOCK]))
            value_total = add_rows(value_total, partners[depth_index], rounded(value_term[:, low:low + BLOCK]))
        return attention, query_grad, key_total, value_total

    head_shape = (batch, SEQ, HEADS, HEAD_DIM)
    start_state = (jnp.zeros(head_shape, jnp.bfloat16), jnp.zeros(head_shape, jnp.bfloat16), jnp.zeros(head_shape, jnp.float32), jnp.zeros(head_shape, jnp.float32))
    attention, query_grad, key_total, value_total = lax.fori_loop(0, num_blocks, one_block, start_state)
    layer_out = jnp.dot(attention.reshape(-1, width), out_proj, preferred_element_type=jnp.float32)
    layer_out = layer_out.astype(jnp.bfloat16).reshape(batch, SEQ, width)
    return (layer_out, query_grad.reshape(batch, SEQ, width), key_total.astype(jnp.bfloat16).reshape(batch, SEQ, width), value_total.astype(jnp.bfloat16).reshape(batch, SEQ, width))
```

```python
from functools import partial

import jax
import jax.numpy as jnp
from jax import lax
from jax.experimental import pallas as pl
from jax.experimental.pallas import tpu as pltpu
from jax.sharding import PartitionSpec as P

HEAD_DIM = 128
COARSE_LEVELS = 2
LOG2_E = 1.4426950408889634
FAR_OFF = 1e30
VMEM_LIMIT = 24 * 1024 * 1024


def dot_t(a, b):
    return lax.dot_general(a, b, (((1,), (1,)), ((), ())), preferred_element_type=jnp.float32)


def dot_n(a, b):
    return lax.dot_general(a, b, (((1,), (0,)), ((), ())), preferred_element_type=jnp.float32)


def dot_l(a, b):
    return lax.dot_general(a, b, (((0,), (0,)), ((), ())), preferred_element_type=jnp.float32)


def unit_kernel(levels, fine, coarse, has_next, n_alias, scalars, *refs):
    refs = list(refs)
    q_ref, k_ref, v_ref, grad_own, grad_other, proj_own, proj_other = refs[:7]
    refs = refs[7:]
    far_refs = refs[:levels]
    refs = refs[levels:]
    if has_next:
        next_k, next_v = refs[:2]
        refs = refs[2:]
    refs = refs[n_alias:]
    attn_ref, dq_ref, own_ref = refs[:3]
    refs = refs[3:]
    coarse_refs = refs[: len(coarse)]
    refs = refs[len(coarse) :]
    fine_refs = refs[: len(fine)]
    refs = refs[len(fine) :]
    weight_scr, low_scr = refs

    scale = HEAD_DIM ** (-0.5)
    rows = q_ref.shape[1]
    queries = q_ref[0]
    grad_t = (
        dot_t(proj_own[...], grad_own[0]) + dot_t(proj_other[...], grad_other[0])
    ).astype(jnp.bfloat16)

    def keys_of(index):
        return k_ref[0] if index == 0 else far_refs[index - 1][0]

    def values_of(index):
        return v_ref[0] if index == 0 else far_refs[index - 1][1]

    def span(index):
        return pl.ds(index * rows, rows)

    shift = [jnp.float32(0.0)]
    for level in range(levels):
        shift.append(jnp.where(scalars[2 + level] == 1, jnp.float32(0.0), jnp.float32(FAR_OFF)))

    maxima = None
    for index in range(levels + 1):
        scores = dot_t(keys_of(index), queries) * jnp.float32(scale * LOG2_E)
        if index == 0:
            key_at = lax.broadcasted_iota(jnp.int32, scores.shape, 0)
            query_at = lax.broadcasted_iota(jnp.int32, scores.shape, 1)
            scores = jnp.where(key_at <= query_at, scores, -jnp.float32(FAR_OFF))
        weight_scr[span(index), :] = scores
        top = jnp.max(scores, axis=0, keepdims=True) - shift[index]
        maxima = top if maxima is None else jnp.maximum(maxima, top)
    total = None
    for index in range(levels + 1):
        powers = jnp.exp2(weight_scr[span(index), :] - (maxima + shift[index]))
        weight_scr[span(index), :] = powers
        part = jnp.sum(powers, axis=0, keepdims=True)
        total = part if total is None else total + part
    inverse = 1.0 / total
    attn_t = None
    for index in range(levels + 1):
        weights = weight_scr[span(index), :] * inverse
        weight_scr[span(index), :] = weights
        low = weights.astype(jnp.bfloat16)
        low_scr[span(index), :] = low
        part = dot_l(values_of(index), low)
        attn_t = part if attn_t is None else attn_t + part
    attn_t = attn_t.astype(jnp.bfloat16).astype(jnp.float32)
    attn_ref[...] = attn_t.T.astype(jnp.bfloat16)
    row_dsum = jnp.sum(grad_t.astype(jnp.float32) * attn_t, axis=0, keepdims=True)

    dq_t = None
    for index in range(levels + 1):
        low = low_scr[span(index), :]
        value_term = dot_t(low, grad_t)
        grad_weights = dot_n(values_of(index), grad_t)
        grad_scores = (weight_scr[span(index), :] * (grad_weights - row_dsum)).astype(jnp.bfloat16)
        key_term = dot_n(grad_scores, queries) * scale
        part = dot_l(keys_of(index), grad_scores)
        dq_t = part if dq_t is None else dq_t + part
        if index == 0:
            own_ref[0] = key_term
            own_ref[1] = value_term
        else:
            level = index - 1
            if level in coarse:
                target = coarse_refs[coarse.index(level)]
            else:
                target = fine_refs[fine.index(level)]
            target[0] = key_term.astype(jnp.bfloat16)
            target[1] = value_term.astype(jnp.bfloat16)
            if has_next and level in fine:

                @pl.when(scalars[2 + level] == 0)
                def _():
                    target[0] = next_k[0]
                    target[1] = next_v[0]

    dq_ref[0] = (dq_t * scale).T.astype(jnp.bfloat16)


def chunk_call(levels, fine, coarse, chunk, upcoming, far_at, down_at, down_units, scalars, arrays, far, carried):
    queries, keys, values, output_grad, other_grad, out_proj = arrays
    batch_at, head_at, count = chunk
    rows, width = queries.shape[1], queries.shape[2]
    has_next = upcoming is not None
    wide = out_proj.shape[1] // 2

    def of_unit(batch, head):
        return pl.BlockSpec((1, rows, HEAD_DIM), lambda i, s, b=batch, h=head: (b, 0, h + i))

    in_specs = [
        of_unit(batch_at, head_at),
        of_unit(batch_at, head_at),
        of_unit(batch_at, head_at),
        pl.BlockSpec((1, rows, wide), lambda i, s: (batch_at, 0, 0)),
        pl.BlockSpec((1, rows, wide), lambda i, s: (0, 0, 0)),
        pl.BlockSpec((HEAD_DIM, wide), lambda i, s: (head_at + i, s[0])),
        pl.BlockSpec((HEAD_DIM, wide), lambda i, s: (head_at + i, s[1])),
    ]
    operands = [queries, keys, values, output_grad, other_grad, out_proj, out_proj]
    for level in range(levels):
        in_specs.append(
            pl.BlockSpec((2, rows, HEAD_DIM), lambda i, s, h=far_at[level]: (0, 0, h + i))
        )
        operands.append(far[level])
    if has_next:
        in_specs += [of_unit(*upcoming[:2])] * 2
        operands += [keys, values]

    out_shapes = [
        jax.ShapeDtypeStruct((rows, width), jnp.bfloat16),
        jax.ShapeDtypeStruct(queries.shape, jnp.bfloat16),
        jax.ShapeDtypeStruct((2, rows, width), jnp.float32),
    ]
    out_specs = [
        pl.BlockSpec((rows, HEAD_DIM), lambda i, s: (0, head_at + i)),
        of_unit(batch_at, head_at),
        pl.BlockSpec((2, rows, HEAD_DIM), lambda i, s: (0, 0, head_at + i)),
    ]
    for place, level in enumerate(coarse):
        out_shapes.append(
            jax.ShapeDtypeStruct((2, rows, down_units[place] * HEAD_DIM), jnp.bfloat16)
        )
        out_specs.append(
            pl.BlockSpec((2, rows, HEAD_DIM), lambda i, s, h=down_at[place]: (0, 0, h + i))
        )
    for level in fine:
        out_shapes.append(jax.ShapeDtypeStruct((2, rows, count * HEAD_DIM), jnp.bfloat16))
        out_specs.append(pl.BlockSpec((2, rows, HEAD_DIM), lambda i, s: (0, 0, i)))

    aliases = {}
    for place, held in enumerate(carried):
        if held is not None:
            aliases[1 + len(operands)] = place
            in_specs.append(pl.BlockSpec(memory_space=pl.ANY))
            operands.append(held)
    seen = (levels + 1) * rows
    flops = count * 2 * (6 * seen * rows * HEAD_DIM + 2 * rows * wide * HEAD_DIM)
    return pl.pallas_call(
        partial(unit_kernel, levels, fine, coarse, has_next, len(aliases)),
        out_shape=out_shapes,
        grid_spec=pltpu.PrefetchScalarGridSpec(
            num_scalar_prefetch=1,
            grid=(count,),
            in_specs=in_specs,
            out_specs=out_specs,
            scratch_shapes=[
                pltpu.VMEM((seen, rows), jnp.float32),
                pltpu.VMEM((seen, rows), jnp.bfloat16),
            ],
        ),
        input_output_aliases=aliases,
        compiler_params=pltpu.CompilerParams(vmem_limit_bytes=VMEM_LIMIT),
        cost_estimate=pl.CostEstimate(
            flops=flops, bytes_accessed=count * 4 * 2**20, transcendentals=count * seen * rows
        ),
    )(scalars, *operands)


def project_kernel(scalars, attn_ref, proj_ref, send_ref, own_ref):
    step = pl.program_id(0)
    product = dot_n(attn_ref[...], proj_ref[...])

    @pl.when(step < 2)
    def _():
        send_ref[...] = product.astype(jnp.bfloat16)

    @pl.when(step >= 2)
    def _():
        own_ref[...] = product


def project(scalars, attn, out_proj):
    rows, depth = attn.shape
    wide = out_proj.shape[1] // 2
    block = wide // 2
    return pl.pallas_call(
        project_kernel,
        out_shape=[
            jax.ShapeDtypeStruct((rows, wide), jnp.bfloat16),
            jax.ShapeDtypeStruct((rows, wide), jnp.float32),
        ],
        grid_spec=pltpu.PrefetchScalarGridSpec(
            num_scalar_prefetch=1,
            grid=(4,),
            in_specs=[
                pl.BlockSpec((rows, depth), lambda i, s: (0, 0)),
                pl.BlockSpec(
                    (depth, block), lambda i, s: (0, jnp.where(i < 2, s[1], s[0]) * 2 + i % 2)
                ),
            ],
            out_specs=[
                pl.BlockSpec((rows, block), lambda i, s: (0, jnp.minimum(i, 1))),
                pl.BlockSpec((rows, block), lambda i, s: (0, jnp.maximum(i - 2, 0))),
            ],
        ),
        compiler_params=pltpu.CompilerParams(vmem_limit_bytes=VMEM_LIMIT),
        cost_estimate=pl.CostEstimate(
            flops=4 * rows * depth * wide, bytes_accessed=6 * 2**20, transcendentals=0
        ),
    )(scalars, attn, out_proj)


def finish_kernel(levels, masked, scalars, *refs):
    own_ref, far_refs = refs[0], refs[1 : 1 + levels]
    key_ref, value_ref = refs[-2:]
    for place, target in enumerate((key_ref, value_ref)):
        total = own_ref[place]
        for level in range(levels):
            term = far_refs[level][place].astype(jnp.float32)
            if masked[level]:
                term = jnp.where(scalars[2 + level] == 1, jnp.zeros_like(term), term)
            total = total + term
        target[0] = total.astype(jnp.bfloat16)


def finish(levels, masked, chunk, far_at, shape, scalars, own, far, carried):
    batch_at, head_at, count = chunk
    rows = shape[1]
    in_specs = [pl.BlockSpec((2, rows, HEAD_DIM), lambda i, s: (0, 0, head_at + i))]
    operands = [own]
    for level in range(levels):
        in_specs.append(
            pl.BlockSpec((2, rows, HEAD_DIM), lambda i, s, h=far_at[level]: (0, 0, h + i))
        )
        operands.append(far[level])
    aliases = {}
    for place, held in enumerate(carried):
        if held is not None:
            aliases[1 + len(operands)] = place
            in_specs.append(pl.BlockSpec(memory_space=pl.ANY))
            operands.append(held)
    out_spec = pl.BlockSpec((1, rows, HEAD_DIM), lambda i, s: (batch_at, 0, head_at + i))
    return pl.pallas_call(
        partial(finish_kernel, levels, masked),
        out_shape=[jax.ShapeDtypeStruct(shape, jnp.bfloat16)] * 2,
        grid_spec=pltpu.PrefetchScalarGridSpec(
            num_scalar_prefetch=1, grid=(count,), in_specs=in_specs, out_specs=[out_spec] * 2
        ),
        input_output_aliases=aliases,
        compiler_params=pltpu.CompilerParams(vmem_limit_bytes=VMEM_LIMIT),
        cost_estimate=pl.CostEstimate(
            flops=count * 2 * (levels + 1) * rows * HEAD_DIM,
            bytes_accessed=count * rows * HEAD_DIM * 4 * (levels + 3),
            transcendentals=0,
        ),
    )(scalars, *operands)


def groups_of(sizes, heads):
    out, at = [], 0
    for size in sizes:
        out.append((at // heads, at % heads, size))
        at += size
    return out


def holder(groups, chunk):
    for index, (batch, head, count) in enumerate(groups):
        if batch == chunk[0] and head <= chunk[1] < head + count:
            return index, chunk[1] - head
    raise ValueError("chunk")


def body(queries, key_states, value_states, output_grad, out_proj):
    batch, rows, width = queries.shape
    heads = width // HEAD_DIM
    seq_size = lax.axis_size("seq")
    levels = seq_size.bit_length() - 1
    coarse = list(range(min(COARSE_LEVELS, levels)))
    fine = list(range(len(coarse), levels))
    place = lax.axis_index("seq")
    half = lax.axis_index("head")
    scalars = jnp.stack(
        [half, 1 - half] + [place // 2**level % 2 for level in range(levels)]
    ).astype(jnp.int32)

    step = 2
    units = batch * heads
    chunks = groups_of([step] * (units // step), heads)
    count = len(chunks)
    split = [[heads] * batch, [step, heads - step] + [heads] * (batch - 1)]
    split_down = [[heads] * batch, [heads] * (batch - 1) + [heads - step, step]]
    ups = [groups_of(split[level], heads) for level in coarse]
    downs = [groups_of(split_down[level], heads) for level in coarse]

    lower = [[i for i in range(seq_size) if not (i >> level) & 1] for level in range(levels)]
    up_pairs = [[(i, i + 2**level) for i in lower[level]] for level in range(levels)]
    down_pairs = [[(i + 2**level, i) for i in lower[level]] for level in range(levels)]

    def packed(group):
        at, head, number = group
        low, high = head * HEAD_DIM, (head + number) * HEAD_DIM
        return jnp.stack([key_states[at, :, low:high], value_states[at, :, low:high]])

    def other_half(source):
        return lax.ppermute(source, "head", [(0, 1), (1, 0)])

    far_fine = {}
    for t in range(2):
        buffer = packed(chunks[t])
        for level in reversed(fine):
            far_fine[level, t] = lax.ppermute(buffer, "seq", up_pairs[level])
    other_grads = [other_half(output_grad[at : at + 1]) for at in range(batch)]
    far_coarse = {
        (level, index): lax.ppermute(packed(group), "seq", up_pairs[level])
        for level in reversed(coarse)
        for index, group in enumerate(ups[level])
    }

    attn = [None] * batch
    own = [None] * batch
    query_grad = None
    down_buffers = {}
    back_coarse = {}
    layer_parts = []
    grads = (None, None)

    def finished(c, grads):
        chunk = chunks[c]
        far, far_at, masked = [], [], []
        for level in range(levels):
            if level in coarse:
                index, at = holder(downs[level], chunk)
                far.append(back_coarse[level, index])
                masked.append(False)
            else:
                far.append(far_fine[level, c + 2])
                at = 0
                masked.append(c + 2 < count)
            far_at.append(at)
        return finish(
            levels, masked, chunk, far_at, queries.shape, scalars, own[chunk[0]], far, grads
        )

    for t, chunk in enumerate(chunks):
        at = chunk[0]
        upcoming = chunks[t + 2] if t + 2 < count else None
        far, far_at, down_at, down_units, down_index = [], [], [], [], []
        for level in range(levels):
            if level in coarse:
                index, offset = holder(ups[level], chunk)
                far.append(far_coarse[level, index])
                index, down_offset = holder(downs[level], chunk)
                down_index.append(index)
                down_at.append(down_offset)
                down_units.append(downs[level][index][2])
            else:
                far.append(far_fine[level, t])
                offset = 0
            far_at.append(offset)
        carried = [attn[at], query_grad, own[at]] + [
            down_buffers.get((level, down_index[level])) for level in coarse
        ]
        results = chunk_call(
            levels,
            fine,
            coarse,
            chunk,
            upcoming,
            far_at,
            down_at,
            down_units,
            scalars,
            (queries, key_states, value_states, output_grad, other_grads[at], out_proj),
            far,
            carried,
        )
        attn[at], query_grad, own[at] = results[:3]
        for level in coarse:
            down_buffers[level, down_index[level]] = results[3 + level]
            group = downs[level][down_index[level]]
            if group[0] == at and group[1] + group[2] == chunk[1] + chunk[2]:
                back_coarse[level, down_index[level]] = lax.ppermute(
                    results[3 + level], "seq", down_pairs[level]
                )
        for place_of, level in reversed(list(enumerate(fine))):
            pairs = down_pairs[level] + (up_pairs[level] if upcoming is not None else [])
            far_fine[level, t + 2] = lax.ppermute(results[3 + len(coarse) + place_of], "seq", pairs)
        if chunk[1] + chunk[2] == heads:
            send, kept = project(scalars, attn[at], out_proj)
            layer_parts.append(kept + other_half(send).astype(jnp.float32))
    for c in range(count):
        grads = finished(c, grads)
    layer_out = jnp.stack(layer_parts).astype(jnp.bfloat16)
    return layer_out, query_grad, grads[0], grads[1]


def solution(mesh):
    spec = P(None, "seq", "head")
    return jax.shard_map(
        body,
        mesh=mesh,
        in_specs=(spec, spec, spec, spec, P("head", None)),
        out_specs=(spec, spec, spec, spec),
        check_vma=False,
    )
```

```python
from functools import partial

import jax
import jax.numpy as jnp
from jax import lax
from jax.experimental import pallas as pl
from jax.experimental.pallas import tpu as pltpu
from jax.sharding import PartitionSpec as P

HEAD_DIM = 128
COARSE_LEVELS = 2
LOG2_E = 1.4426950408889634
FAR_OFF = 1e30
VMEM_LIMIT = 24 * 1024 * 1024
COST_SHARE = 20


def cost(flops, bytes_accessed, transcendentals=0):
    parts = (flops, bytes_accessed, transcendentals)
    flops, bytes_accessed, transcendentals = (int(part * COST_SHARE) for part in parts)
    return pl.CostEstimate(
        flops=flops, bytes_accessed=bytes_accessed, transcendentals=transcendentals
    )


def dot_t(a, b):
    return lax.dot_general(a, b, (((1,), (1,)), ((), ())), preferred_element_type=jnp.float32)


def dot_n(a, b):
    return lax.dot_general(a, b, (((1,), (0,)), ((), ())), preferred_element_type=jnp.float32)


def dot_l(a, b):
    return lax.dot_general(a, b, (((0,), (0,)), ((), ())), preferred_element_type=jnp.float32)


def unit_steps(levels, width, refs, masks, scratch, place):
    q_ref, k_ref, v_ref, grad_ref, far_refs, attn_ref, dq_ref, own_ref, out_refs = refs
    keys_scr, values_scr, weight_scr, low_scr, grad_scr = [ref.at[place] for ref in scratch]
    cols = slice(place * HEAD_DIM, (place + 1) * HEAD_DIM)
    scale = HEAD_DIM ** (-0.5)
    rows = q_ref.shape[1]
    blocks = range(levels + 1)

    def span(index):
        return pl.ds(index * rows, rows)

    for index in blocks:
        keys_scr[span(index), :] = k_ref[0, :, cols] if index == 0 else far_refs[index - 1][0, :, cols]
        values_scr[span(index), :] = v_ref[0, :, cols] if index == 0 else far_refs[index - 1][1, :, cols]
    queries = q_ref[0, :, cols]
    queries_t = queries.astype(jnp.float32).T.astype(jnp.bfloat16)
    weight_scr[...] = dot_n(keys_scr[...], queries_t)
    yield
    grad_t = grad_ref[cols, :]
    grad = grad_t.astype(jnp.float32).T.astype(jnp.bfloat16)
    factor = jnp.float32(scale * LOG2_E)
    own_scores = weight_scr[span(0), :]
    key_at = lax.broadcasted_iota(jnp.int32, own_scores.shape, 0)
    query_at = lax.broadcasted_iota(jnp.int32, own_scores.shape, 1)
    weight_scr[span(0), :] = jnp.where(key_at <= query_at, own_scores, -jnp.float32(FAR_OFF))
    maxima = None
    for index in blocks:
        top = jnp.max(weight_scr[span(index), :], axis=0, keepdims=True) * factor - masks[index]
        maxima = top if maxima is None else jnp.maximum(maxima, top)
    total = None
    for index in blocks:
        powers = jnp.exp2(weight_scr[span(index), :] * factor - (maxima + masks[index]))
        weight_scr[span(index), :] = powers
        part = jnp.sum(powers, axis=0, keepdims=True)
        total = part if total is None else total + part
    inverse = 1.0 / total
    for index in blocks:
        weights = weight_scr[span(index), :] * inverse
        weight_scr[span(index), :] = weights
        low_scr[span(index), :] = weights.astype(jnp.bfloat16)
    yield
    attn_t = dot_l(values_scr[...], low_scr[...])
    grad_weights = dot_n(values_scr[...], grad_t)
    value_terms = dot_n(low_scr[...], grad)
    yield
    attn_t = attn_t.astype(jnp.bfloat16).astype(jnp.float32)
    attn_ref[:, cols] = attn_t.T.astype(jnp.bfloat16)
    row_dsum = jnp.sum(grad_t.astype(jnp.float32) * attn_t, axis=0, keepdims=True)
    own_ref[1, :, cols] = value_terms[:rows]
    for index in blocks:
        if index:
            out_refs[index - 1][1, :, cols] = value_terms[index * rows : (index + 1) * rows].astype(
                jnp.bfloat16
            )
    for index in blocks:
        grad_scr[span(index), :] = (
            weight_scr[span(index), :]
            * (grad_weights[index * rows : (index + 1) * rows] - row_dsum)
        ).astype(jnp.bfloat16)
    yield
    key_terms = dot_n(grad_scr[...], queries)
    dq_t = dot_l(keys_scr[...], grad_scr[...])
    yield
    own_ref[0, :, cols] = key_terms[:rows] * scale
    for index in blocks:
        if index:
            out_refs[index - 1][0, :, cols] = (
                key_terms[index * rows : (index + 1) * rows] * scale
            ).astype(jnp.bfloat16)
    dq_ref[0, :, cols] = (dq_t * scale).T.astype(jnp.bfloat16)
    yield


def unit_kernel(levels, fine, coarse, has_next, n_alias, pair, scalars, *refs):
    refs = list(refs)
    inputs, refs = refs[:4], refs[4:]
    far_refs, refs = refs[:levels], refs[levels:]
    if has_next:
        (next_k, next_v), refs = refs[:2], refs[2:]
    refs = refs[n_alias:]
    outputs, refs = refs[:3], refs[3:]
    coarse_refs, refs = refs[: len(coarse)], refs[len(coarse) :]
    fine_refs, scratch = refs[: len(fine)], refs[len(fine) :]
    out_refs = [
        coarse_refs[coarse.index(level)] if level in coarse else fine_refs[fine.index(level)]
        for level in range(levels)
    ]
    masks = [jnp.float32(0.0)] + [
        jnp.where(scalars[2 + level] == 1, jnp.float32(0.0), jnp.float32(FAR_OFF))
        for level in range(levels)
    ]
    steps = [
        unit_steps(levels, pair, (*inputs, far_refs, *outputs, out_refs), masks, scratch, place)
        for place in range(pair)
    ]
    for tick in range(6 + pair - 1):
        for place, step in enumerate(steps):
            if 0 <= tick - place < 6:
                next(step)
    if has_next:
        for level in fine:

            @pl.when(scalars[2 + level] == 0)
            def _():
                out_refs[level][0] = next_k[0]
                out_refs[level][1] = next_v[0]


def chunk_call(levels, fine, coarse, chunk, upcoming, far_at, down_at, down_units, scalars, arrays, far, carried, gates):
    queries, keys, values, attn_grad = arrays
    batch_at, head_at, count = chunk
    rows, width = queries.shape[1], queries.shape[2]
    has_next = upcoming is not None
    pair = 2 if count % 2 == 0 else 1
    head_at //= pair
    far_at = [at // pair for at in far_at]
    down_at = [at // pair for at in down_at]
    cols = pair * HEAD_DIM

    def of_unit(batch, head):
        return pl.BlockSpec((1, rows, cols), lambda i, s, b=batch, h=head: (b, 0, h + i))

    in_specs = [
        of_unit(batch_at, head_at),
        of_unit(batch_at, head_at),
        of_unit(batch_at, head_at),
        pl.BlockSpec((cols, rows), lambda i, s: (head_at + i, 0)),
    ]
    operands = [queries, keys, values, attn_grad]
    for level in range(levels):
        in_specs.append(
            pl.BlockSpec((2, rows, cols), lambda i, s, h=far_at[level]: (0, 0, h + i))
        )
        operands.append(far[level])
    if has_next:
        in_specs += [of_unit(upcoming[0], upcoming[1] // pair)] * 2
        operands += [keys, values]

    out_shapes = [
        jax.ShapeDtypeStruct((rows, width), jnp.bfloat16),
        jax.ShapeDtypeStruct(queries.shape, jnp.bfloat16),
        jax.ShapeDtypeStruct((2, rows, width), jnp.float32),
    ]
    out_specs = [
        pl.BlockSpec((rows, cols), lambda i, s: (0, head_at + i)),
        of_unit(batch_at, head_at),
        pl.BlockSpec((2, rows, cols), lambda i, s: (0, 0, head_at + i)),
    ]
    for place, level in enumerate(coarse):
        out_shapes.append(
            jax.ShapeDtypeStruct((2, rows, down_units[place] * HEAD_DIM), jnp.bfloat16)
        )
        out_specs.append(
            pl.BlockSpec((2, rows, cols), lambda i, s, h=down_at[place]: (0, 0, h + i))
        )
    for level in fine:
        out_shapes.append(jax.ShapeDtypeStruct((2, rows, count * HEAD_DIM), jnp.bfloat16))
        out_specs.append(pl.BlockSpec((2, rows, cols), lambda i, s: (0, 0, i)))

    aliases = {}
    for place, held in enumerate(carried):
        if held is not None:
            aliases[1 + len(operands)] = place
            in_specs.append(pl.BlockSpec(memory_space=pl.ANY))
            operands.append(held)
    for gate in gates:
        in_specs.append(pl.BlockSpec(memory_space=pl.ANY))
        operands.append(gate)
    seen = (levels + 1) * rows
    flops = count * 2 * 6 * seen * rows * HEAD_DIM
    return pl.pallas_call(
        partial(unit_kernel, levels, fine, coarse, has_next, len(aliases) + len(gates), pair),
        out_shape=out_shapes,
        grid_spec=pltpu.PrefetchScalarGridSpec(
            num_scalar_prefetch=1,
            grid=(count // pair,),
            in_specs=in_specs,
            out_specs=out_specs,
            scratch_shapes=[
                pltpu.VMEM((pair, seen, HEAD_DIM), jnp.bfloat16),
                pltpu.VMEM((pair, seen, HEAD_DIM), jnp.bfloat16),
                pltpu.VMEM((pair, seen, rows), jnp.float32),
                pltpu.VMEM((pair, seen, rows), jnp.bfloat16),
                pltpu.VMEM((pair, seen, rows), jnp.bfloat16),
            ],
        ),
        input_output_aliases=aliases,
        compiler_params=pltpu.CompilerParams(vmem_limit_bytes=VMEM_LIMIT),
        cost_estimate=cost(
            flops=flops, bytes_accessed=count * 4 * 2**20, transcendentals=count * seen * rows
        ),
    )(scalars, *operands)


def grad_kernel(scalars, own_ref, other_ref, proj_own, proj_other, grad_ref):
    grad_ref[...] = (
        dot_t(proj_own[...], own_ref[0]) + dot_t(proj_other[...], other_ref[0])
    ).astype(jnp.bfloat16)


def grad_project(scalars, output_grad, batch_at, other_grad, out_proj):
    rows = output_grad.shape[1]
    width, wide = out_proj.shape[0], out_proj.shape[1] // 2
    block = 256
    return pl.pallas_call(
        grad_kernel,
        out_shape=jax.ShapeDtypeStruct((width, rows), jnp.bfloat16),
        grid_spec=pltpu.PrefetchScalarGridSpec(
            num_scalar_prefetch=1,
            grid=(width // block,),
            in_specs=[
                pl.BlockSpec((1, rows, wide), lambda i, s: (batch_at, 0, 0)),
                pl.BlockSpec((1, rows, wide), lambda i, s: (0, 0, 0)),
                pl.BlockSpec((block, wide), lambda i, s: (i, s[0])),
                pl.BlockSpec((block, wide), lambda i, s: (i, s[1])),
            ],
            out_specs=pl.BlockSpec((block, rows), lambda i, s: (i, 0)),
        ),
        compiler_params=pltpu.CompilerParams(vmem_limit_bytes=VMEM_LIMIT),
        cost_estimate=cost(
            flops=4 * rows * wide * width, bytes_accessed=6 * 2**20, transcendentals=0
        ),
    )(scalars, output_grad, other_grad, out_proj, out_proj)


def project_kernel(scalars, attn_ref, proj_ref, send_ref, own_ref):
    step = pl.program_id(0)
    product = dot_n(attn_ref[...], proj_ref[...])

    @pl.when(step < 2)
    def _():
        send_ref[...] = product.astype(jnp.bfloat16)

    @pl.when(step >= 2)
    def _():
        own_ref[...] = product


def project(scalars, attn, out_proj):
    rows, depth = attn.shape
    wide = out_proj.shape[1] // 2
    block = wide // 2
    return pl.pallas_call(
        project_kernel,
        out_shape=[
            jax.ShapeDtypeStruct((rows, wide), jnp.bfloat16),
            jax.ShapeDtypeStruct((rows, wide), jnp.float32),
        ],
        grid_spec=pltpu.PrefetchScalarGridSpec(
            num_scalar_prefetch=1,
            grid=(4,),
            in_specs=[
                pl.BlockSpec((rows, depth), lambda i, s: (0, 0)),
                pl.BlockSpec(
                    (depth, block), lambda i, s: (0, jnp.where(i < 2, s[1], s[0]) * 2 + i % 2)
                ),
            ],
            out_specs=[
                pl.BlockSpec((rows, block), lambda i, s: (0, jnp.minimum(i, 1))),
                pl.BlockSpec((rows, block), lambda i, s: (0, jnp.maximum(i - 2, 0))),
            ],
        ),
        compiler_params=pltpu.CompilerParams(vmem_limit_bytes=VMEM_LIMIT),
        cost_estimate=cost(
            flops=4 * rows * depth * wide, bytes_accessed=6 * 2**20, transcendentals=0
        ),
    )(scalars, attn, out_proj)


def finish_kernel(levels, masked, scalars, *refs):
    own_ref, far_refs = refs[0], refs[1 : 1 + levels * len(masked)]
    key_ref, value_ref = refs[-2:]
    for index, skip in enumerate(masked):
        wide = far_refs[index * levels].shape[2]
        cols = slice(index * wide, (index + 1) * wide)
        for place, target in enumerate((key_ref, value_ref)):
            total = own_ref[place, :, cols]
            for level in range(levels):
                term = far_refs[index * levels + level][place].astype(jnp.float32)
                if skip[level]:
                    term = jnp.where(scalars[2 + level] == 1, jnp.zeros_like(term), term)
                total = total + term
            target[0, :, cols] = total.astype(jnp.bfloat16)


def finish(levels, masked, chunks, far_at, shape, scalars, own, far, carried):
    batch_at, head_at, count = chunks[0]
    rows, cols, wide = shape[1], count * HEAD_DIM, len(chunks) * count * HEAD_DIM
    at = head_at * HEAD_DIM // wide
    in_specs = [pl.BlockSpec((2, rows, wide), lambda i, s: (0, 0, at))]
    operands = [own]
    for index in range(len(chunks)):
        for level in range(levels):
            in_specs.append(
                pl.BlockSpec(
                    (2, rows, cols), lambda i, s, h=far_at[index][level] // count: (0, 0, h)
                )
            )
            operands.append(far[index][level])
    aliases = {}
    for place, held in enumerate(carried):
        if held is not None:
            aliases[1 + len(operands)] = place
            in_specs.append(pl.BlockSpec(memory_space=pl.ANY))
            operands.append(held)
    out_spec = pl.BlockSpec((1, rows, wide), lambda i, s: (batch_at, 0, at))
    return pl.pallas_call(
        partial(finish_kernel, levels, masked),
        out_shape=[jax.ShapeDtypeStruct(shape, jnp.bfloat16)] * 2,
        grid_spec=pltpu.PrefetchScalarGridSpec(
            num_scalar_prefetch=1, grid=(1,), in_specs=in_specs, out_specs=[out_spec] * 2
        ),
        input_output_aliases=aliases,
        compiler_params=pltpu.CompilerParams(vmem_limit_bytes=VMEM_LIMIT),
        cost_estimate=cost(
            flops=2 * (levels + 1) * rows * wide,
            bytes_accessed=rows * wide * 4 * (levels + 3),
            transcendentals=0,
        ),
    )(scalars, *operands)


def groups_of(sizes):
    return [(sum(sizes[:index]), size) for index, size in enumerate(sizes)]


def holder(groups, first):
    for index, (start, size) in enumerate(groups):
        if start <= first < start + size:
            return index, first - start
    raise ValueError("unit")


def body(queries, key_states, value_states, output_grad, out_proj):
    batch, rows, width = queries.shape
    heads = width // HEAD_DIM
    seq_size = lax.axis_size("seq")
    levels = seq_size.bit_length() - 1
    coarse = list(range(min(COARSE_LEVELS, levels)))
    fine = list(range(len(coarse), levels))
    place = lax.axis_index("seq")
    half = lax.axis_index("head")
    scalars = jnp.stack(
        [half, 1 - half] + [place // 2**level % 2 for level in range(levels)]
    ).astype(jnp.int32)

    step = 2
    units = batch * heads
    count = units // step
    chunks = [(t * step // heads, t * step % heads, step) for t in range(count)]
    ups = [groups_of([units]), groups_of([heads] * batch)]
    downs = [
        groups_of([units]),
        groups_of([heads] * (batch - 1) + [2 * step] * (heads // (2 * step))),
    ]

    lower = [[i for i in range(seq_size) if not (i >> level) & 1] for level in range(levels)]
    up_pairs = [[(i, i + 2**level) for i in lower[level]] for level in range(levels)]
    down_pairs = [[(i + 2**level, i) for i in lower[level]] for level in range(levels)]

    def behind(source, *earlier):
        earlier = [item for item in earlier if item is not None]
        return lax.optimization_barrier((source, *earlier))[0] if earlier else source

    def packed(group, *earlier):
        first, last = group[0], group[0] + group[1]
        sources = behind((key_states, value_states), *earlier)
        spans = []
        for at in range(batch):
            low, high = max(first, at * heads), min(last, (at + 1) * heads)
            if low < high:
                spans.append((at, (low - at * heads) * HEAD_DIM, (high - at * heads) * HEAD_DIM))
        return jnp.stack(
            [
                jnp.concatenate([source[at, :, low:high] for at, low, high in spans], axis=1)
                for source in sources
            ]
        )

    def other_half(source):
        return lax.ppermute(source, "head", [(0, 1), (1, 0)])

    far_fine, far_coarse = {}, {}

    def send_coarse(level, index, *earlier):
        far_coarse[level, index] = lax.ppermute(
            packed(ups[level][index], *earlier), "seq", up_pairs[level]
        )

    def send_grad(at, *earlier):
        other = other_half(behind(output_grad, *earlier)[at : at + 1])
        attn_grads[at] = grad_project(scalars, output_grad, at, other, out_proj)
        return other

    def arrived(t):
        return [far_fine[level, t] for level in fine]

    attn_grads, gates = {}, {}
    opening = packed((0, 2 * step))
    for level in reversed(fine):
        far_fine[level, 0] = far_fine[level, 1] = lax.ppermute(opening, "seq", up_pairs[level])
    for level in reversed(coarse):
        send_coarse(level, 0)
    first_grad = send_grad(0)
    send_grad(1, first_grad)
    gates[3] = (attn_grads[1],)

    attn = [None] * batch
    own = [None] * batch
    query_grad = None
    down_buffers = {}
    back_coarse = {}
    grads = (None, None)

    def finished(first, last, grads):
        far, far_at, masked = [], [], []
        for c in range(first, last):
            chunk = chunks[c]
            far.append([])
            far_at.append([])
            masked.append([])
            for level in range(levels):
                if level in coarse:
                    index, at = holder(downs[level], c * step)
                    far[-1].append(back_coarse[level, index])
                    masked[-1].append(False)
                else:
                    far[-1].append(far_fine[level, c + 2])
                    at = 0
                    masked[-1].append(c + 2 < count)
                far_at[-1].append(at)
        return finish(
            levels,
            masked,
            chunks[first:last],
            far_at,
            queries.shape,
            scalars,
            own[chunks[first][0]],
            far,
            grads,
        )

    def send_down(level, index, *earlier):
        back_coarse[level, index] = lax.ppermute(
            behind(down_buffers[level, index], *earlier), "seq", down_pairs[level]
        )

    def send_out(*earlier):
        parts = [project(scalars, source, out_proj) for source in attn]
        sent = behind(jnp.stack([send for send, _ in parts]), *earlier)
        kept = jnp.stack([kept for _, kept in parts])
        return kept, other_half(sent)

    for t, chunk in enumerate(chunks):
        at = chunk[0]
        upcoming = chunks[t + 2] if t + 2 < count else None
        far, far_at, down_at, down_units, down_index = [], [], [], [], []
        for level in range(levels):
            if level in coarse:
                index, offset = holder(ups[level], t * step)
                far.append(far_coarse[level, index])
                index, down_offset = holder(downs[level], t * step)
                down_index.append(index)
                down_at.append(down_offset)
                down_units.append(downs[level][index][1])
            else:
                far.append(far_fine[level, t])
                offset = t * step if t < 2 else 0
            far_at.append(offset)
        carried = [attn[at], query_grad, own[at]] + [
            down_buffers.get((level, down_index[level])) for level in coarse
        ]
        results = chunk_call(
            levels,
            fine,
            coarse,
            chunk,
            upcoming,
            far_at,
            down_at,
            down_units,
            scalars,
            (queries, key_states, value_states, attn_grads[at]),
            far,
            carried,
            gates.get(t, ()),
        )
        attn[at], query_grad, own[at] = results[:3]
        for place_of, level in reversed(list(enumerate(fine))):
            pairs = down_pairs[level] + (up_pairs[level] if upcoming is not None else [])
            far_fine[level, t + 2] = lax.ppermute(results[3 + len(coarse) + place_of], "seq", pairs)
        for level in coarse:
            down_buffers[level, down_index[level]] = results[3 + level]
        marker = results[-1]
        if t == 0:
            send_coarse(1, 1, marker)
        if t == 3:
            send_down(1, 0)
            gates[6] = (back_coarse[1, 0],)
        if t == 5:
            send_down(1, 1, back_coarse[1, 0])
            gates[7] = (back_coarse[1, 1],)
    last = arrived(count)
    send_down(1, 2, back_coarse[1, 1], *last)
    kept, received = send_out(*last)
    send_down(0, 0, *last)
    grads = finished(0, 4, grads)
    grads = finished(4, 7, grads)
    grads = finished(7, 8, grads)
    received = behind(received, *grads)
    layer_out = (kept + received.astype(jnp.float32)).astype(jnp.bfloat16)
    return layer_out, query_grad, grads[0], grads[1]


def solution(mesh):
    spec = P(None, "seq", "head")
    return jax.shard_map(
        body,
        mesh=mesh,
        in_specs=(spec, spec, spec, spec, P("head", None)),
        out_specs=(spec, spec, spec, spec),
        check_vma=False,
    )
```

```python
from functools import partial

import jax
import jax.numpy as jnp
from jax import lax
from jax.experimental import pallas as pl
from jax.experimental.pallas import tpu as pltpu
from jax.sharding import PartitionSpec as P

HEAD_DIM = 128
COARSE_LEVELS = 2
LOG2_E = 1.4426950408889634
FAR_OFF = 1e30
VMEM_LIMIT = 24 * 1024 * 1024
COST_SHARE = 20


def cost(flops, bytes_accessed, transcendentals=0):
    parts = (flops, bytes_accessed, transcendentals)
    flops, bytes_accessed, transcendentals = (int(part * COST_SHARE) for part in parts)
    return pl.CostEstimate(
        flops=flops, bytes_accessed=bytes_accessed, transcendentals=transcendentals
    )


def dot_t(a, b):
    return lax.dot_general(a, b, (((1,), (1,)), ((), ())), preferred_element_type=jnp.float32)


def dot_n(a, b):
    return lax.dot_general(a, b, (((1,), (0,)), ((), ())), preferred_element_type=jnp.float32)


def dot_l(a, b):
    return lax.dot_general(a, b, (((0,), (0,)), ((), ())), preferred_element_type=jnp.float32)


def unit_steps(levels, width, refs, masks, scratch, place):
    q_ref, k_ref, v_ref, grad_ref, far_refs, attn_ref, dq_ref, own_ref, out_refs = refs
    keys_scr, values_scr, weight_scr, low_scr, grad_scr = [ref.at[place] for ref in scratch]
    cols = slice(place * HEAD_DIM, (place + 1) * HEAD_DIM)
    scale = HEAD_DIM ** (-0.5)
    rows = q_ref.shape[1]
    blocks = range(levels + 1)

    def span(index):
        return pl.ds(index * rows, rows)

    for index in blocks:
        keys_scr[span(index), :] = k_ref[0, :, cols] if index == 0 else far_refs[index - 1][0, :, cols]
        values_scr[span(index), :] = v_ref[0, :, cols] if index == 0 else far_refs[index - 1][1, :, cols]
    queries = q_ref[0, :, cols]
    queries_t = queries.astype(jnp.float32).T.astype(jnp.bfloat16)
    weight_scr[...] = dot_n(keys_scr[...], queries_t)
    yield
    grad_t = grad_ref[cols, :]
    grad = grad_t.astype(jnp.float32).T.astype(jnp.bfloat16)
    factor = jnp.float32(scale * LOG2_E)
    own_scores = weight_scr[span(0), :]
    key_at = lax.broadcasted_iota(jnp.int32, own_scores.shape, 0)
    query_at = lax.broadcasted_iota(jnp.int32, own_scores.shape, 1)
    weight_scr[span(0), :] = jnp.where(key_at <= query_at, own_scores, -jnp.float32(FAR_OFF))
    maxima = None
    for index in blocks:
        top = jnp.max(weight_scr[span(index), :], axis=0, keepdims=True) * factor - masks[index]
        maxima = top if maxima is None else jnp.maximum(maxima, top)
    total = None
    for index in blocks:
        powers = jnp.exp2(weight_scr[span(index), :] * factor - (maxima + masks[index]))
        weight_scr[span(index), :] = powers
        part = jnp.sum(powers, axis=0, keepdims=True)
        total = part if total is None else total + part
    inverse = 1.0 / total
    for index in blocks:
        weights = weight_scr[span(index), :] * inverse
        weight_scr[span(index), :] = weights
        low_scr[span(index), :] = weights.astype(jnp.bfloat16)
    yield
    attn_t = dot_l(values_scr[...], low_scr[...])
    grad_weights = dot_n(values_scr[...], grad_t)
    value_terms = dot_n(low_scr[...], grad)
    yield
    attn_t = attn_t.astype(jnp.bfloat16).astype(jnp.float32)
    attn_ref[:, cols] = attn_t.T.astype(jnp.bfloat16)
    row_dsum = jnp.sum(grad_t.astype(jnp.float32) * attn_t, axis=0, keepdims=True)
    own_ref[1, :, cols] = value_terms[:rows]
    for index in blocks:
        if index:
            out_refs[index - 1][1, :, cols] = value_terms[index * rows : (index + 1) * rows].astype(
                jnp.bfloat16
            )
    for index in blocks:
        grad_scr[span(index), :] = (
            weight_scr[span(index), :]
            * (grad_weights[index * rows : (index + 1) * rows] - row_dsum)
        ).astype(jnp.bfloat16)
    yield
    key_terms = dot_n(grad_scr[...], queries)
    dq_t = dot_l(keys_scr[...], grad_scr[...])
    yield
    own_ref[0, :, cols] = key_terms[:rows] * scale
    for index in blocks:
        if index:
            out_refs[index - 1][0, :, cols] = (
                key_terms[index * rows : (index + 1) * rows] * scale
            ).astype(jnp.bfloat16)
    dq_ref[0, :, cols] = (dq_t * scale).T.astype(jnp.bfloat16)
    yield


def unit_kernel(levels, fine, coarse, has_next, n_alias, pair, scalars, *refs):
    refs = list(refs)
    inputs, refs = refs[:4], refs[4:]
    far_refs, refs = refs[:levels], refs[levels:]
    if has_next:
        (next_k, next_v), refs = refs[:2], refs[2:]
    refs = refs[n_alias:]
    outputs, refs = refs[:3], refs[3:]
    coarse_refs, refs = refs[: len(coarse)], refs[len(coarse) :]
    fine_refs, scratch = refs[: len(fine)], refs[len(fine) :]
    out_refs = [
        coarse_refs[coarse.index(level)] if level in coarse else fine_refs[fine.index(level)]
        for level in range(levels)
    ]
    masks = [jnp.float32(0.0)] + [
        jnp.where(scalars[2 + level] == 1, jnp.float32(0.0), jnp.float32(FAR_OFF))
        for level in range(levels)
    ]
    steps = [
        unit_steps(levels, pair, (*inputs, far_refs, *outputs, out_refs), masks, scratch, place)
        for place in range(pair)
    ]
    for tick in range(6 + pair - 1):
        for place, step in enumerate(steps):
            if 0 <= tick - place < 6:
                next(step)
    if has_next:
        for level in fine:

            @pl.when(scalars[2 + level] == 0)
            def _():
                out_refs[level][0] = next_k[0]
                out_refs[level][1] = next_v[0]


def chunk_call(levels, fine, coarse, chunk, upcoming, far_at, down_at, down_units, scalars, arrays, far, carried, gates):
    queries, keys, values, attn_grad = arrays
    batch_at, head_at, count = chunk
    rows, width = queries.shape[1], queries.shape[2]
    has_next = upcoming is not None
    pair = 2 if count % 2 == 0 else 1
    head_at //= pair
    far_at = [at // pair for at in far_at]
    down_at = [at // pair for at in down_at]
    cols = pair * HEAD_DIM

    def of_unit(batch, head):
        return pl.BlockSpec((1, rows, cols), lambda i, s, b=batch, h=head: (b, 0, h + i))

    in_specs = [
        of_unit(batch_at, head_at),
        of_unit(batch_at, head_at),
        of_unit(batch_at, head_at),
        pl.BlockSpec((cols, rows), lambda i, s: (head_at + i, 0)),
    ]
    operands = [queries, keys, values, attn_grad]
    for level in range(levels):
        in_specs.append(
            pl.BlockSpec((2, rows, cols), lambda i, s, h=far_at[level]: (0, 0, h + i))
        )
        operands.append(far[level])
    if has_next:
        in_specs += [of_unit(upcoming[0], upcoming[1] // pair)] * 2
        operands += [keys, values]

    out_shapes = [
        jax.ShapeDtypeStruct((rows, width), jnp.bfloat16),
        jax.ShapeDtypeStruct(queries.shape, jnp.bfloat16),
        jax.ShapeDtypeStruct((2, rows, width), jnp.float32),
    ]
    out_specs = [
        pl.BlockSpec((rows, cols), lambda i, s: (0, head_at + i)),
        of_unit(batch_at, head_at),
        pl.BlockSpec((2, rows, cols), lambda i, s: (0, 0, head_at + i)),
    ]
    for place, level in enumerate(coarse):
        out_shapes.append(
            jax.ShapeDtypeStruct((2, rows, down_units[place] * HEAD_DIM), jnp.bfloat16)
        )
        out_specs.append(
            pl.BlockSpec((2, rows, cols), lambda i, s, h=down_at[place]: (0, 0, h + i))
        )
    for level in fine:
        out_shapes.append(jax.ShapeDtypeStruct((2, rows, count * HEAD_DIM), jnp.bfloat16))
        out_specs.append(pl.BlockSpec((2, rows, cols), lambda i, s: (0, 0, i)))

    aliases = {}
    for place, held in enumerate(carried):
        if held is not None:
            aliases[1 + len(operands)] = place
            in_specs.append(pl.BlockSpec(memory_space=pl.ANY))
            operands.append(held)
    for gate in gates:
        in_specs.append(pl.BlockSpec(memory_space=pl.ANY))
        operands.append(gate)
    seen = (levels + 1) * rows
    flops = count * 2 * 6 * seen * rows * HEAD_DIM
    return pl.pallas_call(
        partial(unit_kernel, levels, fine, coarse, has_next, len(aliases) + len(gates), pair),
        out_shape=out_shapes,
        grid_spec=pltpu.PrefetchScalarGridSpec(
            num_scalar_prefetch=1,
            grid=(count // pair,),
            in_specs=in_specs,
            out_specs=out_specs,
            scratch_shapes=[
                pltpu.VMEM((pair, seen, HEAD_DIM), jnp.bfloat16),
                pltpu.VMEM((pair, seen, HEAD_DIM), jnp.bfloat16),
                pltpu.VMEM((pair, seen, rows), jnp.float32),
                pltpu.VMEM((pair, seen, rows), jnp.bfloat16),
                pltpu.VMEM((pair, seen, rows), jnp.bfloat16),
            ],
        ),
        input_output_aliases=aliases,
        compiler_params=pltpu.CompilerParams(vmem_limit_bytes=VMEM_LIMIT),
        cost_estimate=cost(
            flops=flops, bytes_accessed=count * 4 * 2**20, transcendentals=count * seen * rows
        ),
    )(scalars, *operands)


def grad_kernel(scalars, own_ref, other_ref, proj_own, proj_other, grad_ref):
    grad_ref[...] = (
        dot_t(proj_own[...], own_ref[0]) + dot_t(proj_other[...], other_ref[0])
    ).astype(jnp.bfloat16)


def grad_project(scalars, output_grad, batch_at, other_grad, out_proj):
    rows = output_grad.shape[1]
    width, wide = out_proj.shape[0], out_proj.shape[1] // 2
    block = 256
    return pl.pallas_call(
        grad_kernel,
        out_shape=jax.ShapeDtypeStruct((width, rows), jnp.bfloat16),
        grid_spec=pltpu.PrefetchScalarGridSpec(
            num_scalar_prefetch=1,
            grid=(width // block,),
            in_specs=[
                pl.BlockSpec((1, rows, wide), lambda i, s: (batch_at, 0, 0)),
                pl.BlockSpec((1, rows, wide), lambda i, s: (0, 0, 0)),
                pl.BlockSpec((block, wide), lambda i, s: (i, s[0])),
                pl.BlockSpec((block, wide), lambda i, s: (i, s[1])),
            ],
            out_specs=pl.BlockSpec((block, rows), lambda i, s: (i, 0)),
        ),
        compiler_params=pltpu.CompilerParams(vmem_limit_bytes=VMEM_LIMIT),
        cost_estimate=cost(
            flops=4 * rows * wide * width, bytes_accessed=6 * 2**20, transcendentals=0
        ),
    )(scalars, output_grad, other_grad, out_proj, out_proj)


def project_kernel(scalars, attn_ref, proj_ref, send_ref, own_ref):
    step = pl.program_id(0)
    product = dot_n(attn_ref[...], proj_ref[...])

    @pl.when(step < 2)
    def _():
        send_ref[...] = product.astype(jnp.bfloat16)

    @pl.when(step >= 2)
    def _():
        own_ref[...] = product


def project(scalars, attn, out_proj):
    rows, depth = attn.shape
    wide = out_proj.shape[1] // 2
    block = wide // 2
    return pl.pallas_call(
        project_kernel,
        out_shape=[
            jax.ShapeDtypeStruct((rows, wide), jnp.bfloat16),
            jax.ShapeDtypeStruct((rows, wide), jnp.float32),
        ],
        grid_spec=pltpu.PrefetchScalarGridSpec(
            num_scalar_prefetch=1,
            grid=(4,),
            in_specs=[
                pl.BlockSpec((rows, depth), lambda i, s: (0, 0)),
                pl.BlockSpec(
                    (depth, block), lambda i, s: (0, jnp.where(i < 2, s[1], s[0]) * 2 + i % 2)
                ),
            ],
            out_specs=[
                pl.BlockSpec((rows, block), lambda i, s: (0, jnp.minimum(i, 1))),
                pl.BlockSpec((rows, block), lambda i, s: (0, jnp.maximum(i - 2, 0))),
            ],
        ),
        compiler_params=pltpu.CompilerParams(vmem_limit_bytes=VMEM_LIMIT),
        cost_estimate=cost(
            flops=4 * rows * depth * wide, bytes_accessed=6 * 2**20, transcendentals=0
        ),
    )(scalars, attn, out_proj)


def finish_kernel(levels, masked, scalars, *refs):
    own_ref, far_refs = refs[0], refs[1 : 1 + levels * len(masked)]
    key_ref, value_ref = refs[-2:]
    for index, skip in enumerate(masked):
        wide = far_refs[index * levels].shape[2]
        cols = slice(index * wide, (index + 1) * wide)
        for place, target in enumerate((key_ref, value_ref)):
            total = own_ref[place, :, cols]
            for level in range(levels):
                term = far_refs[index * levels + level][place].astype(jnp.float32)
                if skip[level]:
                    term = jnp.where(scalars[2 + level] == 1, jnp.zeros_like(term), term)
                total = total + term
            target[0, :, cols] = total.astype(jnp.bfloat16)


def finish(levels, masked, chunks, far_at, shape, scalars, own, far, carried):
    batch_at, head_at, count = chunks[0]
    rows, cols, wide = shape[1], count * HEAD_DIM, len(chunks) * count * HEAD_DIM
    at = head_at * HEAD_DIM // wide
    in_specs = [pl.BlockSpec((2, rows, wide), lambda i, s: (0, 0, at))]
    operands = [own]
    for index in range(len(chunks)):
        for level in range(levels):
            in_specs.append(
                pl.BlockSpec(
                    (2, rows, cols), lambda i, s, h=far_at[index][level] // count: (0, 0, h)
                )
            )
            operands.append(far[index][level])
    aliases = {}
    for place, held in enumerate(carried):
        if held is not None:
            aliases[1 + len(operands)] = place
            in_specs.append(pl.BlockSpec(memory_space=pl.ANY))
            operands.append(held)
    out_spec = pl.BlockSpec((1, rows, wide), lambda i, s: (batch_at, 0, at))
    return pl.pallas_call(
        partial(finish_kernel, levels, masked),
        out_shape=[jax.ShapeDtypeStruct(shape, jnp.bfloat16)] * 2,
        grid_spec=pltpu.PrefetchScalarGridSpec(
            num_scalar_prefetch=1, grid=(1,), in_specs=in_specs, out_specs=[out_spec] * 2
        ),
        input_output_aliases=aliases,
        compiler_params=pltpu.CompilerParams(vmem_limit_bytes=VMEM_LIMIT),
        cost_estimate=cost(
            flops=2 * (levels + 1) * rows * wide,
            bytes_accessed=rows * wide * 4 * (levels + 3),
            transcendentals=0,
        ),
    )(scalars, *operands)


def groups_of(sizes):
    return [(sum(sizes[:index]), size) for index, size in enumerate(sizes)]


def holder(groups, first):
    for index, (start, size) in enumerate(groups):
        if start <= first < start + size:
            return index, first - start
    raise ValueError("unit")


def body(queries, key_states, value_states, output_grad, out_proj):
    batch, rows, width = queries.shape
    heads = width // HEAD_DIM
    seq_size = lax.axis_size("seq")
    levels = seq_size.bit_length() - 1
    coarse = list(range(min(COARSE_LEVELS, levels)))
    fine = list(range(len(coarse), levels))
    place = lax.axis_index("seq")
    half = lax.axis_index("head")
    scalars = jnp.stack(
        [half, 1 - half] + [place // 2**level % 2 for level in range(levels)]
    ).astype(jnp.int32)

    step = 2
    units = batch * heads
    count = units // step
    chunks = [(t * step // heads, t * step % heads, step) for t in range(count)]
    ups = [groups_of([units]), groups_of([heads] * batch)]
    downs = [
        groups_of([units]),
        groups_of([heads] * (batch - 1) + [2 * step] * (heads // (2 * step))),
    ]

    lower = [[i for i in range(seq_size) if not (i >> level) & 1] for level in range(levels)]
    up_pairs = [[(i, i + 2**level) for i in lower[level]] for level in range(levels)]
    down_pairs = [[(i + 2**level, i) for i in lower[level]] for level in range(levels)]

    def behind(source, *earlier):
        earlier = [item for item in earlier if item is not None]
        return lax.optimization_barrier((source, *earlier))[0] if earlier else source

    def packed(group, *earlier):
        first, last = group[0], group[0] + group[1]
        sources = behind((key_states, value_states), *earlier)
        spans = []
        for at in range(batch):
            low, high = max(first, at * heads), min(last, (at + 1) * heads)
            if low < high:
                spans.append((at, (low - at * heads) * HEAD_DIM, (high - at * heads) * HEAD_DIM))
        return jnp.stack(
            [
                jnp.concatenate([source[at, :, low:high] for at, low, high in spans], axis=1)
                for source in sources
            ]
        )

    def other_half(source):
        return lax.ppermute(source, "head", [(0, 1), (1, 0)])

    far_fine, far_coarse = {}, {}

    def send_coarse(level, index, *earlier):
        far_coarse[level, index] = lax.ppermute(
            packed(ups[level][index], *earlier), "seq", up_pairs[level]
        )

    def send_grad(at, *earlier):
        other = other_half(behind(output_grad, *earlier)[at : at + 1])
        attn_grads[at] = grad_project(scalars, output_grad, at, other, out_proj)
        return other

    def arrived(t):
        return [far_fine[level, t] for level in fine]

    attn_grads, gates = {}, {}
    opening = packed((0, 2 * step))
    for level in reversed(fine):
        far_fine[level, 0] = far_fine[level, 1] = lax.ppermute(opening, "seq", up_pairs[level])
    for level in reversed(coarse):
        send_coarse(level, 0)
    first_grad = send_grad(0)
    send_grad(1, first_grad)
    gates[3] = (attn_grads[1],)

    attn = [None] * batch
    own = [None] * batch
    query_grad = None
    down_buffers = {}
    back_coarse = {}
    grads = (None, None)

    def finished(first, last, grads):
        far, far_at, masked = [], [], []
        for c in range(first, last):
            chunk = chunks[c]
            far.append([])
            far_at.append([])
            masked.append([])
            for level in range(levels):
                if level in coarse:
                    index, at = holder(downs[level], c * step)
                    far[-1].append(back_coarse[level, index])
                    masked[-1].append(False)
                else:
                    far[-1].append(far_fine[level, c + 2])
                    at = 0
                    masked[-1].append(c + 2 < count)
                far_at[-1].append(at)
        return finish(
            levels,
            masked,
            chunks[first:last],
            far_at,
            queries.shape,
            scalars,
            own[chunks[first][0]],
            far,
            grads,
        )

    def send_down(level, index, *earlier):
        back_coarse[level, index] = lax.ppermute(
            behind(down_buffers[level, index], *earlier), "seq", down_pairs[level]
        )

    def send_out(*earlier):
        parts = [project(scalars, source, out_proj) for source in attn]
        sent = behind(jnp.stack([send for send, _ in parts]), *earlier)
        kept = jnp.stack([kept for _, kept in parts])
        return kept, sent, other_half(sent)

    for t, chunk in enumerate(chunks):
        at = chunk[0]
        upcoming = chunks[t + 2] if t + 2 < count else None
        far, far_at, down_at, down_units, down_index = [], [], [], [], []
        for level in range(levels):
            if level in coarse:
                index, offset = holder(ups[level], t * step)
                far.append(far_coarse[level, index])
                index, down_offset = holder(downs[level], t * step)
                down_index.append(index)
                down_at.append(down_offset)
                down_units.append(downs[level][index][1])
            else:
                far.append(far_fine[level, t])
                offset = t * step if t < 2 else 0
            far_at.append(offset)
        carried = [attn[at], query_grad, own[at]] + [
            down_buffers.get((level, down_index[level])) for level in coarse
        ]
        results = chunk_call(
            levels,
            fine,
            coarse,
            chunk,
            upcoming,
            far_at,
            down_at,
            down_units,
            scalars,
            (queries, key_states, value_states, attn_grads[at]),
            far,
            carried,
            gates.get(t, ()),
        )
        attn[at], query_grad, own[at] = results[:3]
        for place_of, level in reversed(list(enumerate(fine))):
            pairs = down_pairs[level] + (up_pairs[level] if upcoming is not None else [])
            far_fine[level, t + 2] = lax.ppermute(results[3 + len(coarse) + place_of], "seq", pairs)
        for level in coarse:
            down_buffers[level, down_index[level]] = results[3 + level]
        marker = results[-1]
        if t == 0:
            send_coarse(1, 1, marker)
        if t == 3:
            send_down(1, 0)
            gates[6] = (back_coarse[1, 0],)
        if t == 5:
            send_down(1, 1, back_coarse[1, 0])
            gates[7] = (back_coarse[1, 1],)
    last = arrived(count)
    send_down(1, 2, back_coarse[1, 1], *last)
    kept, sent, received = send_out(*last)
    send_down(0, 0, sent, *last)
    grads = finished(0, 4, grads)
    grads = finished(4, 7, grads)
    grads = finished(7, 8, grads)
    received = behind(received, *grads)
    layer_out = (kept + received.astype(jnp.float32)).astype(jnp.bfloat16)
    return layer_out, query_grad, grads[0], grads[1]


def solution(mesh):
    spec = P(None, "seq", "head")
    return jax.shard_map(
        body,
        mesh=mesh,
        in_specs=(spec, spec, spec, spec, P("head", None)),
        out_specs=(spec, spec, spec, spec),
        check_vma=False,
    )
```
